256 devices in a mesh: tok: 32 (over x, z_hi, y), feat: 8 (over z_lo, core).
Axes of the slice: x: 4, y: 4, z: 8 (z_hi: 2, z_lo: 4; z = z_hi * 4 + z_lo), core: 2. Of those that a mesh axis runs over, the one named last changes fastest.
Arguments:
- activations: bfloat16 [65536, 16384], P('tok', 'feat'), may hold values from -6 to 6
- probes: bfloat16 [256, 16384], P(None, 'feat'), may hold values from -6 to 6
Outputs:
- first_product: float32 [256, 16384], P('tok', 'feat')
- second_product: float32 [256, 16384], P('tok', 'feat')
The draws below stay inside these ranges and needn't reach their ends.
All inputs are finite; a program needn't handle non-finite values.
Results may differ from the reference program's by a relative error of at most 0.0027.
Values may be sent and summed in bfloat16 or wider, within the bound.
No kernel may reach another device: no remote copies, remote signals or barrier semaphores. Data moves between devices by JAX's collectives and lax.ppermute only.
A program may use at most 64 MiB of HBM per device.

```python
import jax
import jax.numpy as jnp

F = 16384
P_SIZE = 256
TOKENS = 65536


def shard_levels(own_key, extent, split, smallest, top_value):
    gain, own = 1.0, jax.random.fold_in(own_key, 6)
    for position, blocks in split:
        steps = jnp.exp(jax.random.uniform(jax.random.fold_in(own, position), (blocks,), jnp.float32, smallest / len(split), top_value / len(split)))
        gain = gain * jnp.repeat(steps, extent[position] // blocks).reshape([-1 if axis == position else 1 for axis in range(len(extent))])
    return gain


def normal_values(key, extent, deviation, bound, shards=(), held_as=jnp.bfloat16):
    array = deviation * jax.random.normal(key, extent, jnp.float32)
    if shards:
        array = array * shard_levels(key, extent, shards, -0.22, 0.18)
    return jnp.clip(array, -bound, bound).astype(held_as)


def setup_inputs(seed: int = 0) -> dict:
    key_list = jax.random.split(jax.random.key(seed), 3)
    activations = normal_values(key_list[0], (TOKENS, F), 1.0, 6.0, ((0, 32), (1, 8)))
    probes = normal_values(key_list[1], (P_SIZE, F), 1.0, 6.0, ((1, 8),))
    return {"activations": activations, "probes": probes}


def reference(activations, probes):
    token_scores = jnp.dot(activations, probes.T, preferred_element_type=jnp.float32).astype(jnp.bfloat16)
    first_product = jnp.dot(token_scores.T, activations, preferred_element_type=jnp.float32) / TOKENS
    first_rounded = first_product.astype(jnp.bfloat16)
    second_scores = jnp.dot(activations, first_rounded.T, preferred_element_type=jnp.float32).astype(jnp.bfloat16)
    second_product = jnp.dot(second_scores.T, activations, preferred_element_type=jnp.float32) / TOKENS
    return first_product, second_product
```

```python
import jax
import jax.numpy as jnp
from jax import lax
from jax.experimental import pallas as pl
from jax.experimental.pallas import tpu as pltpu
from jax.sharding import Mesh, PartitionSpec as P

SIZES = {"x": 4, "h": 2, "y": 4, "z": 4, "c": 2}
F32, BF16 = jnp.float32, jnp.bfloat16


def dot(a, b, dim_a, dim_b):
    return lax.dot_general(
        a, b, (((dim_a,), (dim_b,)), ((), ())), preferred_element_type=F32
    )


def send(value, axis, step):
    n = SIZES[axis]
    return lax.ppermute(value, axis, [(i, (i + step) % n) for i in range(n)])


def scatter(parts, axis):
    got = [send(part.astype(BF16), axis, d) for d, part in enumerate(parts) if d]
    total = parts[0].astype(F32)
    for part in got:
        total = total + part.astype(F32)
    return total


def gather(part, axis):
    return [part] + [send(part, axis, -d) for d in range(1, SIZES[axis])]


def load_and_score(activations, probes, other_core, out_type):
    rows, features = activations.shape
    block = rows // 8

    def kernel(x_hbm, p_ref, x_ref, s_ref, sems):
        core, z = lax.axis_index("c"), lax.axis_index("z")
        half = 1 - core if other_core else core

        def copy(i):
            start = pl.multiple_of((half * 4 + lax.rem(z + i, 4)) * block, block)
            return pltpu.make_async_copy(
                x_hbm.at[pl.ds(start, block)],
                x_ref.at[pl.ds(i * block, block)],
                sems.at[i],
            )

        for i in range(4):
            copy(i).start()
        for i in range(4):
            copy(i).wait()
            own = pl.ds(i * block, block)
            s_ref[own] = dot(x_ref[own], p_ref[...], 1, 1).astype(s_ref.dtype)

    return pl.pallas_call(
        kernel,
        in_specs=[
            pl.BlockSpec(memory_space=pl.ANY),
            pl.BlockSpec(memory_space=pltpu.VMEM),
        ],
        out_specs=[pl.BlockSpec(memory_space=pltpu.VMEM)] * 2,
        out_shape=[
            pltpu.VMEM((rows // 2, features), BF16),
            pltpu.VMEM((rows // 2, probes.shape[0]), out_type),
        ],
        scratch_shapes=[pltpu.SemaphoreType.DMA((4,))],
        compiler_params=pltpu.CompilerParams(vmem_limit_bytes=24 * 2**20),
        cost_estimate=pl.CostEstimate(
            flops=rows * features * probes.shape[0],
            bytes_accessed=rows * features,
            transcendentals=0,
        ),
    )(activations, probes)


def sum_scores(theirs, own):
    total = own + send(theirs.astype(BF16), "c", 1).astype(F32)
    block = total.shape[0] // 4
    parts = [total[d * block : (d + 1) * block] for d in range(4)]
    mine = scatter(parts, "z").astype(BF16)
    half = jnp.concatenate(gather(mine, "z"), 0)
    return send(half, "c", 1), half


def reduce_tokens(x_theirs, x_own, s_theirs, s_own):
    term = dot(s_own, x_own, 0, 0) + dot(s_theirs, x_theirs, 0, 0)
    features = term.shape[1]
    term = term.reshape(4, 2, 4, -1, features)
    cut = features // 2
    a, b = term[..., :cut], term[..., cut:]
    a = scatter([a[d] for d in range(4)], "x")
    b = scatter([b[:, :, d] for d in range(4)], "y")
    a = scatter([a[:, d] for d in range(4)], "y")
    b = scatter([b[d] for d in range(4)], "x")
    return jnp.concatenate([a, b], -1)


def shards(activations, probes):
    x, h, y = (lax.axis_index(name) for name in ("x", "h", "y"))
    features = probes.shape[1]
    total_tokens = activations.shape[0] * 32
    rolled = probes.reshape(4, 2, 4, -1, features)
    rolled = lax.dynamic_slice_in_dim(jnp.concatenate([rolled] * 2, 0), x, 4, 0)
    rolled = lax.dynamic_slice_in_dim(jnp.concatenate([rolled] * 2, 2), y, 4, 2)
    rolled = rolled.reshape(probes.shape)

    x_theirs, s_theirs = load_and_score(activations, rolled, True, BF16)
    x_own, s_own = load_and_score(activations, rolled, False, F32)
    s_theirs, s_own = sum_scores(s_theirs, s_own)

    rows = reduce_tokens(x_theirs, x_own, s_theirs, s_own)
    rows = (rows + send(rows.astype(BF16), "h", 1).astype(F32)) / total_tokens
    first = lax.dynamic_index_in_dim(rows, h, 0, keepdims=False)

    rounded = rows.astype(BF16)
    cut = features // 2
    a = jnp.stack(gather(rounded[..., :cut], "y"), 1)
    b = jnp.stack(gather(rounded[..., cut:], "x"), 0)
    a = jnp.stack(gather(a, "x"), 0)
    b = jnp.stack(gather(b, "y"), 2)
    full = jnp.concatenate([a, b], -1).reshape(probes.shape)

    t_theirs = dot(x_theirs, full, 1, 1)
    t_own = dot(x_own, full, 1, 1)
    t_theirs, t_own = sum_scores(t_theirs, t_own)
    rows = reduce_tokens(x_theirs, x_own, t_theirs, t_own)
    mine = lax.dynamic_index_in_dim(rows, h, 0, keepdims=False)
    other = lax.dynamic_index_in_dim(rows, 1 - h, 0, keepdims=False)
    second = (mine + send(other.astype(BF16), "h", 1).astype(F32)) / total_tokens
    return first, second


def solution(mesh):
    split = Mesh(mesh.devices.reshape(tuple(SIZES.values())), tuple(SIZES))
    tok, feat = ("x", "h", "y"), ("z", "c")
    return jax.shard_map(
        shards,
        mesh=split,
        in_specs=(P(tok, feat), P(None, feat)),
        out_specs=(P(tok, feat), P(tok, feat)),
        check_vma=False,
    )
```

```python
import jax
import jax.numpy as jnp
from jax import lax
from jax.experimental import pallas as pl
from jax.experimental.pallas import tpu as pltpu
from jax.sharding import Mesh, PartitionSpec as P

SIZES = {"x": 4, "h": 2, "y": 4, "z": 4, "c": 2}
F32, BF16 = jnp.float32, jnp.bfloat16
VMEM = pl.BlockSpec(memory_space=pltpu.VMEM)
TILE = 512

ROWS = 16
PIECES = 2


def dot(a, b, dim_a, dim_b):
    return lax.dot_general(
        a, b, (((dim_a,), (dim_b,)), ((), ())), preferred_element_type=F32
    )


def place(index, outer, inner):
    return lax.bitwise_xor(index, outer ^ 3 * inner)


def swap(value, axis, mask):
    return lax.ppermute(value, axis, [(i, i ^ mask) for i in range(SIZES[axis])])


def swap_xy(value, stage, bits):
    pairs = []
    for x in range(4):
        for y in range(4):
            for c in range(2):
                unit = 1 if c == stage else 3
                to = (x ^ bits // 2 * unit) * 4 + (y ^ bits % 2 * unit)
                pairs.append(((x * 4 + y) * 2 + c, to * 2 + c))
    return lax.ppermute(value, ("x", "y", "c"), pairs)


def reduce_four(parts, stage, kind):
    total = parts[0].astype(F32)
    for got in [swap_xy(parts[i].astype(kind), stage, i) for i in (3, 1, 2)]:
        total = total + got.astype(F32)
    return total


def gather_four(part, stage):
    got = {i: swap_xy(part, stage, i) for i in (3, 1, 2)}
    return jnp.stack([part, got[1], got[2], got[3]])


def call(kernel, outs, *args, specs=None, scratch=(), flops=0, limit=16):
    return pl.pallas_call(
        kernel,
        in_specs=specs or [VMEM] * len(args),
        out_specs=[VMEM] * len(outs),
        out_shape=[pltpu.VMEM(shape, kind) for shape, kind in outs],
        scratch_shapes=list(scratch),
        compiler_params=pltpu.CompilerParams(vmem_limit_bytes=limit * 2**20),
        cost_estimate=pl.CostEstimate(
            flops=flops, bytes_accessed=2**20, transcendentals=0
        ),
    )(*args)


def token_rows(x_ref):
    parity = lax.rem(lax.axis_index("z"), 2)
    block = x_ref.shape[0] // (2 * PIECES)
    starts = []
    for piece in range(PIECES):
        for chip in (parity, 1 - parity):
            starts.append((chip * PIECES + piece) * block)
    return [pl.ds(pl.multiple_of(start, block), block) for start in starts]


def write_scores(x_ref, probes, s_ref):
    block = x_ref.shape[0] // (2 * PIECES)
    for i, rows in enumerate(token_rows(x_ref)):
        value = dot(x_ref[rows], probes, 1, 1)
        s_ref[pl.ds(i * block, block)] = value.astype(s_ref.dtype)


def load(activations, probes):
    tokens, features = activations.shape
    half, count = tokens // 2, probes.shape[0]

    def kernel(x_hbm, p_hbm, theirs_ref, own_ref, p_ref, s_ref, raw_ref, row_ref, sems):
        core, x, y = (lax.axis_index(name) for name in ("c", "x", "y"))

        def rows_of(c):
            return x_hbm.at[pl.ds(pl.multiple_of(c * half, half), half)]

        copies = [
            pltpu.make_async_copy(p_hbm, raw_ref, sems.at[0]),
            pltpu.make_async_copy(rows_of(1 - core), theirs_ref, sems.at[1]),
            pltpu.make_async_copy(rows_of(core), own_ref, sems.at[2]),
        ]
        for copy in copies:
            copy.start()
        copies[0].wait()
        row_ref[...] = raw_ref[...].astype(F32)
        for i in range(16):
            at_x = place(x, i // 8, i // 2 % 2)
            at_y = place(y, i // 4 % 2, i % 2)
            pair = [
                row_ref[pl.ds(pl.multiple_of(at_x * 64 + h * 32 + at_y * 8, 8), 8)]
                for h in range(2)
            ]
            p_ref[pl.ds(i * ROWS, ROWS)] = jnp.concatenate(pair, 0).astype(BF16)
        copies[1].wait()
        write_scores(theirs_ref, p_ref[...], s_ref)
        copies[2].wait()

    hbm = pl.BlockSpec(memory_space=pltpu.HBM)
    return call(
        kernel,
        [((half, features), BF16)] * 2 + [(probes.shape, BF16), ((half, count), BF16)],
        activations,
        probes,
        specs=[hbm, hbm],
        scratch=[
            pltpu.VMEM(probes.shape, BF16),
            pltpu.VMEM(probes.shape, F32),
            pltpu.SemaphoreType.DMA((3,)),
        ],
        flops=tokens * features * count,
        limit=48,
    )


def score(x_half, probes, out_type):
    tokens, features = x_half.shape

    def kernel(x_ref, p_ref, s_ref):
        write_scores(x_ref, p_ref[...], s_ref)

    return call(
        kernel,
        [((tokens, probes.shape[0]), out_type)],
        x_half,
        probes,
        flops=2 * tokens * features * probes.shape[0],
    )[0]


def add_piece(own, theirs, piece):
    block = own.shape[0] // (2 * PIECES)
    shape = (block, own.shape[1])

    def kernel(own_ref, theirs_ref, kept_ref, given_ref):
        for i, out_ref in enumerate((kept_ref, given_ref)):
            rows = pl.ds((2 * piece + i) * block, block)
            total = own_ref[rows] + theirs_ref[rows].astype(F32)
            out_ref[...] = total.astype(out_ref.dtype)

    return call(kernel, [(shape, F32), (shape, BF16)], own, theirs, flops=2**20)


def add(kept, got, kinds):
    def kernel(kept_ref, got_ref, *out_refs):
        total = kept_ref[...] + got_ref[...].astype(F32)
        for out_ref in out_refs:
            out_ref[...] = total.astype(out_ref.dtype)

    return call(kernel, [(kept.shape, kind) for kind in kinds], kept, got, flops=2**20)


def sum_scores(theirs, own):
    theirs = swap(theirs, "c", 1)
    pieces = []
    for piece in range(PIECES):
        kept, given = add_piece(own, theirs, piece)
        kept, given = add(kept, swap(given, "z", 1), (F32, BF16))
        (mine,) = add(kept, swap(given, "z", 2), (BF16,))
        other = swap(mine, "z", 1)
        pieces.append(((mine, other), (swap(mine, "c", 1), swap(other, "c", 1))))
    return pieces


def product_term(x_refs, s_refs, piece, cols):
    total = None
    for i, s_ref in enumerate(s_refs):
        x_ref = x_refs[i // 2]
        rows = token_rows(x_ref)[2 * piece + i % 2]
        term = dot(s_ref[...], x_ref[rows, cols], 0, 0)
        total = term if total is None else total + term
    return total


def product_part(y_before, x_own, x_theirs, scores, piece):
    features = x_own.shape[1]
    tokens, probes = scores[0].shape

    def kernel(*refs):
        *y_ref, xo_ref, xt_ref, s0_ref, s1_ref, s2_ref, s3_ref, out_ref = refs
        for i in range(0, features, TILE):
            cols = pl.ds(i, TILE)
            term = product_term(
                (xo_ref, xt_ref), (s0_ref, s1_ref, s2_ref, s3_ref), piece, cols
            )
            out_ref[:, cols] = y_ref[0][:, cols] + term if y_ref else term

    return call(
        kernel,
        [((probes, features), F32)],
        *([] if y_before is None else [y_before]),
        x_own,
        x_theirs,
        *scores,
        flops=8 * tokens * features * probes,
    )[0]


def in_order(value, order_a):
    if order_a:
        return value
    return jnp.concatenate(
        [
            value[(j * 4 + i) * ROWS : (j * 4 + i + 1) * ROWS]
            for i in range(4)
            for j in range(4)
        ],
        0,
    )


def product_last(y_before, x_own, x_theirs, scores):
    features = x_own.shape[1]
    tokens, probes = scores[0].shape
    cut = features // 2

    def kernel(*refs):
        y_ref, xo_ref, xt_ref, s0_ref, s1_ref, s2_ref, s3_ref = refs[:7]
        theirs_ref, own_ref, sum_ref = refs[7:]
        core = lax.axis_index("c")
        for i in range(0, features, TILE):
            cols = pl.ds(i, TILE)
            term = product_term(
                (xo_ref, xt_ref), (s0_ref, s1_ref, s2_ref, s3_ref), PIECES - 1, cols
            )
            sum_ref[:, cols] = y_ref[:, cols] + term

        @pl.when(core == 0)
        def _():
            own_ref[...] = in_order(sum_ref[:, pl.ds(0, cut)], True).astype(BF16)
            theirs_ref[...] = in_order(sum_ref[:, pl.ds(cut, cut)], False).astype(BF16)

        @pl.when(core == 1)
        def _():
            own_ref[...] = in_order(sum_ref[:, pl.ds(cut, cut)], False).astype(BF16)
            theirs_ref[...] = in_order(sum_ref[:, pl.ds(0, cut)], True).astype(BF16)

    return call(
        kernel,
        [((probes, cut), BF16)] * 2,
        y_before,
        x_own,
        x_theirs,
        *scores,
        scratch=[pltpu.VMEM((probes, features), F32)],
        flops=8 * tokens * features * probes,
    )


def product(x_theirs, x_own, pieces):
    y = None
    for piece, (own, theirs) in enumerate(pieces[:-1]):
        y = product_part(y, x_own, x_theirs, (*own, *theirs), piece)
    own, theirs = pieces[-1]
    theirs, own = product_last(y, x_own, x_theirs, (*own, *theirs))
    both = jnp.concatenate([own, swap(theirs, "c", 1)], 1)
    total = reduce_four(both.reshape(4, 4 * ROWS, -1), 0, BF16)
    return reduce_four(total.reshape(4, ROWS, -1), 1, F32)


def whole_features(rows, core):
    cut = rows.shape[1] // 2
    own, arrived = rows[:, :cut], swap(rows[:, cut:], "c", 1)
    return jnp.where(
        core == 0,
        jnp.concatenate([own, arrived], 1),
        jnp.concatenate([arrived, own], 1),
    )


def spread(rounded):
    part = gather_four(rounded, 1).reshape(4 * ROWS, -1)
    full = gather_four(part, 0).reshape(16 * ROWS, -1)
    cut = full.shape[1] // 2
    return assemble(full[:, :cut], swap(full[:, cut:], "c", 1))


def assemble(own, arrived):
    probes, cut = own.shape

    def kernel(own_ref, arrived_ref, full_ref):
        core = lax.axis_index("c")

        def write(ref, columns, order_a):
            value = in_order(ref[...].astype(F32), order_a)
            full_ref[:, columns] = value.astype(BF16)

        @pl.when(core == 0)
        def _():
            write(own_ref, pl.ds(0, cut), True)
            write(arrived_ref, pl.ds(cut, cut), False)

        @pl.when(core == 1)
        def _():
            write(own_ref, pl.ds(cut, cut), False)
            write(arrived_ref, pl.ds(0, cut), True)

    return call(kernel, [((probes, 2 * cut), BF16)], own, arrived)[0]


def shards(activations, probes):
    core, h = lax.axis_index("c"), lax.axis_index("h")
    total_tokens = activations.shape[0] * 32

    x_theirs, x_own, mine, theirs = load(activations, probes)
    scores = sum_scores(theirs, score(x_own, mine, F32))
    rows = product(x_theirs, x_own, scores)
    rows = (rows + swap(rows.astype(BF16), "h", 1).astype(F32)) / total_tokens
    first = lax.dynamic_slice_in_dim(rows, h * 8, 8, 0)

    full = spread(rows.astype(BF16))
    theirs = score(x_theirs, full, BF16)
    scores = sum_scores(theirs, score(x_own, full, F32))
    rows = product(x_theirs, x_own, scores)
    mine = lax.dynamic_slice_in_dim(rows, h * 8, 8, 0)
    other = lax.dynamic_slice_in_dim(rows, (1 - h) * 8, 8, 0)
    second = (mine + swap(other, "h", 1)) / total_tokens
    return whole_features(first, core), whole_features(second, core)


def solution(mesh):
    split = Mesh(mesh.devices.reshape(tuple(SIZES.values())), tuple(SIZES))
    tok, feat = ("x", "h", "y"), ("z", "c")
    return jax.shard_map(
        shards,
        mesh=split,
        in_specs=(P(tok, feat), P(None, feat)),
        out_specs=(P(tok, feat), P(tok, feat)),
        check_vma=False,
    )
```

```python
import jax
import jax.numpy as jnp
from jax import lax
from jax.experimental import pallas as pl
from jax.experimental.pallas import tpu as pltpu
from jax.sharding import Mesh, PartitionSpec as P

SIZES = {"x": 4, "h": 2, "y": 4, "z": 4, "c": 2}
F32, BF16 = jnp.float32, jnp.bfloat16
VMEM = pl.BlockSpec(memory_space=pltpu.VMEM)
TILE = 512

ROWS = 16
PIECES = 2


def dot(a, b, dim_a, dim_b):
    return lax.dot_general(
        a, b, (((dim_a,), (dim_b,)), ((), ())), preferred_element_type=F32
    )


def swap(value, axis, mask):
    return lax.ppermute(value, axis, [(i, i ^ mask) for i in range(SIZES[axis])])


def swap_xy(value, stage, bits):
    pairs = []
    for x in range(4):
        for y in range(4):
            for c in range(2):
                to = (x ^ bits) * 4 + y if c == stage else x * 4 + (y ^ bits)
                pairs.append(((x * 4 + y) * 2 + c, to * 2 + c))
    return lax.ppermute(value, ("x", "y", "c"), pairs)


def reduce_four(kept, given, stage):
    total = kept
    for got in [swap_xy(given[i - 1], stage, i) for i in (2, 1, 3)]:
        total = total + got.astype(F32)
    return total


def gather_four(part, stage):
    got = {i: swap_xy(part, stage, i) for i in (2, 1, 3)}
    return jnp.stack([part, got[1], got[2], got[3]])


def call(kernel, outs, *args, specs=None, scratch=(), flops=0, limit=16):
    return pl.pallas_call(
        kernel,
        in_specs=specs or [VMEM] * len(args),
        out_specs=[VMEM] * len(outs),
        out_shape=[pltpu.VMEM(shape, kind) for shape, kind in outs],
        scratch_shapes=list(scratch),
        compiler_params=pltpu.CompilerParams(vmem_limit_bytes=limit * 2**20),
        cost_estimate=pl.CostEstimate(
            flops=flops, bytes_accessed=2**20, transcendentals=0
        ),
    )(*args)


def token_rows(x_ref):
    parity = lax.rem(lax.axis_index("z"), 2)
    block = x_ref.shape[0] // (2 * PIECES)
    starts = []
    for piece in range(PIECES):
        for chip in (parity, 1 - parity):
            starts.append((chip * PIECES + piece) * block)
    return [pl.ds(pl.multiple_of(start, block), block) for start in starts]


def write_scores(x_ref, probes, s_ref):
    block = x_ref.shape[0] // (2 * PIECES)
    for i, rows in enumerate(token_rows(x_ref)):
        value = dot(x_ref[rows], probes, 1, 1)
        s_ref[pl.ds(i * block, block)] = value.astype(s_ref.dtype)


def load(activations, probes):
    tokens, features = activations.shape
    half, count = tokens // 2, probes.shape[0]

    def kernel(x_hbm, p_hbm, theirs_ref, own_ref, p_ref, s_ref, raw_ref, row_ref, sems):
        core, x, y = (lax.axis_index(name) for name in ("c", "x", "y"))

        def rows_of(c):
            return x_hbm.at[pl.ds(pl.multiple_of(c * half, half), half)]

        copies = [
            pltpu.make_async_copy(p_hbm, raw_ref, sems.at[0]),
            pltpu.make_async_copy(rows_of(1 - core), theirs_ref, sems.at[1]),
            pltpu.make_async_copy(rows_of(core), own_ref, sems.at[2]),
        ]
        for copy in copies:
            copy.start()
        copies[0].wait()
        row_ref[...] = raw_ref[...].astype(F32)
        for i in range(16):
            at_x = lax.bitwise_xor(x, i // 4)
            at_y = lax.bitwise_xor(y, i % 4)
            pair = [
                row_ref[pl.ds(pl.multiple_of(at_x * 64 + h * 32 + at_y * 8, 8), 8)]
                for h in range(2)
            ]
            p_ref[pl.ds(i * ROWS, ROWS)] = jnp.concatenate(pair, 0).astype(BF16)
        copies[1].wait()
        write_scores(theirs_ref, p_ref[...], s_ref)
        copies[2].wait()

    hbm = pl.BlockSpec(memory_space=pltpu.HBM)
    return call(
        kernel,
        [((half, features), BF16)] * 2 + [(probes.shape, BF16), ((half, count), BF16)],
        activations,
        probes,
        specs=[hbm, hbm],
        scratch=[
            pltpu.VMEM(probes.shape, BF16),
            pltpu.VMEM(probes.shape, F32),
            pltpu.SemaphoreType.DMA((3,)),
        ],
        flops=tokens * features * count,
        limit=48,
    )


def score(x_half, probes, out_type):
    tokens, features = x_half.shape

    def kernel(x_ref, p_ref, s_ref):
        write_scores(x_ref, p_ref[...], s_ref)

    return call(
        kernel,
        [((tokens, probes.shape[0]), out_type)],
        x_half,
        probes,
        flops=2 * tokens * features * probes.shape[0],
    )[0]


def reorder(ref, out_ref):
    core = lax.axis_index("c")

    @pl.when(core == 0)
    def _():
        out_ref[...] = ref[...]

    @pl.when(core == 1)
    def _():
        blocks = [
            ref[pl.ds((inner * 4 + outer) * ROWS, ROWS)]
            for outer in range(4)
            for inner in range(4)
        ]
        out_ref[...] = jnp.concatenate(blocks, 0)


def in_order_a(rows):
    def kernel(rows_ref, out_ref):
        reorder(rows_ref, out_ref)

    return call(kernel, [(rows.shape, BF16)], rows, flops=2**20)[0]


def add_piece(own, theirs, piece):
    block = own.shape[0] // (2 * PIECES)
    shape = (block, own.shape[1])

    def kernel(own_ref, theirs_ref, kept_ref, given_ref):
        for i, out_ref in enumerate((kept_ref, given_ref)):
            rows = pl.ds((2 * piece + i) * block, block)
            total = own_ref[rows] + theirs_ref[rows].astype(F32)
            out_ref[...] = total.astype(out_ref.dtype)

    return call(kernel, [(shape, F32), (shape, BF16)], own, theirs, flops=2**20)


def add(kept, got, kinds):
    def kernel(kept_ref, got_ref, *out_refs):
        total = kept_ref[...] + got_ref[...].astype(F32)
        for out_ref in out_refs:
            out_ref[...] = total.astype(out_ref.dtype)

    return call(kernel, [(kept.shape, kind) for kind in kinds], kept, got, flops=2**20)


def sum_scores(theirs, own):
    theirs = swap(theirs, "c", 1)
    mine, other = [], []
    for piece in range(PIECES):
        kept, given = add_piece(own, theirs, piece)
        kept, given = add(kept, swap(given, "z", 1), (F32, BF16))
        (whole,) = add(kept, swap(given, "z", 2), (BF16,))
        arrived = swap(whole, "z", 1)
        mine += [whole, swap(whole, "c", 1)]
        other += [arrived, swap(arrived, "c", 1)]
    return mine, other


def product_term(x_refs, s_refs, share, cols):
    total = None
    for i, s_ref in enumerate(s_refs):
        x_ref = x_refs[i % 2]
        rows = token_rows(x_ref)[i // 2 * 2 + share]
        term = dot(s_ref[...], x_ref[rows, cols], 0, 0)
        total = term if total is None else total + term
    return total


def product_mine(x_own, x_theirs, scores):
    features = x_own.shape[1]
    tokens, probes = scores[0].shape

    def kernel(xo_ref, xt_ref, *refs):
        *s_refs, y_ref = refs
        for i in range(0, features, TILE):
            cols = pl.ds(i, TILE)
            y_ref[:, cols] = product_term((xo_ref, xt_ref), s_refs, 0, cols)

    return call(
        kernel,
        [((probes, features), F32)],
        x_own,
        x_theirs,
        *scores,
        flops=2 * len(scores) * tokens * features * probes,
    )[0]


def product_all(y_mine, x_own, x_theirs, scores):
    features = x_own.shape[1]
    tokens, probes = scores[0].shape

    def kernel(y_ref, xo_ref, xt_ref, *refs):
        *s_refs, kept_ref, given_ref, sum_ref, order_ref = refs
        for i in range(0, features, TILE):
            cols = pl.ds(i, TILE)
            term = product_term((xo_ref, xt_ref), s_refs, 1, cols)
            sum_ref[:, cols] = y_ref[:, cols] + term
        reorder(sum_ref, order_ref)
        kept_ref[...] = order_ref[pl.ds(0, probes // 4)]
        for i in range(3):
            rows = pl.ds((i + 1) * (probes // 4), probes // 4)
            given_ref[i] = order_ref[rows].astype(BF16)

    return call(
        kernel,
        [((probes // 4, features), F32), ((3, probes // 4, features), BF16)],
        y_mine,
        x_own,
        x_theirs,
        *scores,
        scratch=[pltpu.VMEM((probes, features), F32)] * 2,
        flops=2 * len(scores) * tokens * features * probes,
    )


def product(x_theirs, x_own, scores):
    mine, other = scores
    y = product_mine(x_own, x_theirs, mine)
    kept, given = product_all(y, x_own, x_theirs, other)
    total = reduce_four(kept, given, 0).reshape(4, ROWS, -1)
    return reduce_four(total[0], total[1:], 1)


def spread(rounded):
    part = gather_four(rounded, 1).reshape(4 * ROWS, -1)
    full = gather_four(part, 0).reshape(16 * ROWS, -1)
    return in_order_a(full)


def shards(activations, probes):
    h = lax.axis_index("h")
    total_tokens = activations.shape[0] * 32

    x_theirs, x_own, mine, theirs = load(activations, probes)
    scores = sum_scores(theirs, score(x_own, mine, F32))
    rows = product(x_theirs, x_own, scores)
    rows = (rows + swap(rows.astype(BF16), "h", 1).astype(F32)) / total_tokens
    first = lax.dynamic_slice_in_dim(rows, h * 8, 8, 0)

    full = spread(rows.astype(BF16))
    theirs = score(x_theirs, full, BF16)
    own = score(x_own, full, F32)
    rows = product(x_theirs, x_own, sum_scores(theirs, own))
    mine = lax.dynamic_slice_in_dim(rows, h * 8, 8, 0)
    other = lax.dynamic_slice_in_dim(rows, (1 - h) * 8, 8, 0)
    return first, (mine + swap(other, "h", 1)) / total_tokens


def solution(mesh):
    split = Mesh(mesh.devices.reshape(tuple(SIZES.values())), tuple(SIZES))
    tok, feat = ("x", "h", "y"), ("z", "c")
    return jax.shard_map(
        shards,
        mesh=split,
        in_specs=(P(tok, feat), P(None, feat)),
        out_specs=(P(tok, feat), P(tok, feat)),
        check_vma=False,
    )
```

```python
import jax
import jax.numpy as jnp
from jax import lax
from jax.experimental import pallas as pl
from jax.experimental.pallas import tpu as pltpu
from jax.sharding import Mesh, PartitionSpec as P

SIZES = {"x": 4, "h": 2, "y": 4, "z": 4, "c": 2}
F32, BF16 = jnp.float32, jnp.bfloat16
VMEM = pl.BlockSpec(memory_space=pltpu.VMEM)
TILE = 512

ROWS = 16
PIECES = 2


def dot(a, b, dim_a, dim_b):
    return lax.dot_general(
        a, b, (((dim_a,), (dim_b,)), ((), ())), preferred_element_type=F32
    )


def swap(value, axis, mask):
    return lax.ppermute(value, axis, [(i, i ^ mask) for i in range(SIZES[axis])])


def swap_xy(value, stage, bits):
    pairs = []
    for x in range(4):
        for y in range(4):
            for c in range(2):
                to = (x ^ bits) * 4 + y if c == stage else x * 4 + (y ^ bits)
                pairs.append(((x * 4 + y) * 2 + c, to * 2 + c))
    return lax.ppermute(value, ("x", "y", "c"), pairs)


def reduce_four(kept, given, stage):
    total = kept
    for got in [swap_xy(given[i - 1], stage, i) for i in (2, 1, 3)]:
        total = total + got.astype(F32)
    return total


def gather_four(part, stage):
    got = {i: swap_xy(part, stage, i) for i in (2, 1, 3)}
    return jnp.stack([part, got[1], got[2], got[3]])


def call(kernel, outs, *args, specs=None, scratch=(), flops=0, limit=16):
    return pl.pallas_call(
        kernel,
        in_specs=specs or [VMEM] * len(args),
        out_specs=[VMEM] * len(outs),
        out_shape=[pltpu.VMEM(shape, kind) for shape, kind in outs],
        scratch_shapes=list(scratch),
        compiler_params=pltpu.CompilerParams(vmem_limit_bytes=limit * 2**20),
        cost_estimate=pl.CostEstimate(
            flops=flops, bytes_accessed=2**20, transcendentals=0
        ),
    )(*args)


def token_rows(x_ref):
    parity = lax.rem(lax.axis_index("z"), 2)
    block = x_ref.shape[0] // (2 * PIECES)
    starts = []
    for piece in range(PIECES):
        for chip in (parity, 1 - parity):
            starts.append((chip * PIECES + piece) * block)
    return [pl.ds(pl.multiple_of(start, block), block) for start in starts]


def write_scores(x_ref, probes, s_ref):
    block = x_ref.shape[0] // (2 * PIECES)
    for i, rows in enumerate(token_rows(x_ref)):
        value = dot(x_ref[rows], probes, 1, 1)
        s_ref[pl.ds(i * block, block)] = value.astype(s_ref.dtype)


def load(activations, probes):
    tokens, features = activations.shape
    half, count = tokens // 2, probes.shape[0]

    def kernel(x_hbm, p_hbm, theirs_ref, own_ref, p_ref, s_ref, raw_ref, row_ref, sems):
        core, x, y = (lax.axis_index(name) for name in ("c", "x", "y"))

        def rows_of(c):
            return x_hbm.at[pl.ds(pl.multiple_of(c * half, half), half)]

        copies = [
            pltpu.make_async_copy(p_hbm, raw_ref, sems.at[0]),
            pltpu.make_async_copy(rows_of(1 - core), theirs_ref, sems.at[1]),
            pltpu.make_async_copy(rows_of(core), own_ref, sems.at[2]),
        ]
        for copy in copies:
            copy.start()
        copies[0].wait()
        row_ref[...] = raw_ref[...].astype(F32)
        for i in range(16):
            at_x = lax.bitwise_xor(x, i // 4)
            at_y = lax.bitwise_xor(y, i % 4)
            pair = [
                row_ref[pl.ds(pl.multiple_of(at_x * 64 + h * 32 + at_y * 8, 8), 8)]
                for h in range(2)
            ]
            p_ref[pl.ds(i * ROWS, ROWS)] = jnp.concatenate(pair, 0).astype(BF16)
        copies[1].wait()
        write_scores(theirs_ref, p_ref[...], s_ref)
        copies[2].wait()

    hbm = pl.BlockSpec(memory_space=pltpu.HBM)
    return call(
        kernel,
        [((half, features), BF16)] * 2 + [(probes.shape, BF16), ((half, count), BF16)],
        activations,
        probes,
        specs=[hbm, hbm],
        scratch=[
            pltpu.VMEM(probes.shape, BF16),
            pltpu.VMEM(probes.shape, F32),
            pltpu.SemaphoreType.DMA((3,)),
        ],
        flops=tokens * features * count,
        limit=48,
    )


def score(x_half, probes, out_type):
    tokens, features = x_half.shape

    def kernel(x_ref, p_ref, s_ref):
        write_scores(x_ref, p_ref[...], s_ref)

    return call(
        kernel,
        [((tokens, probes.shape[0]), out_type)],
        x_half,
        probes,
        flops=2 * tokens * features * probes.shape[0],
    )[0]


def reorder(ref, out_ref):
    core = lax.axis_index("c")

    @pl.when(core == 0)
    def _():
        out_ref[...] = ref[...]

    @pl.when(core == 1)
    def _():
        blocks = [
            ref[pl.ds((inner * 4 + outer) * ROWS, ROWS)]
            for outer in range(4)
            for inner in range(4)
        ]
        out_ref[...] = jnp.concatenate(blocks, 0)


def in_order_a(rows):
    def kernel(rows_ref, out_ref):
        reorder(rows_ref, out_ref)

    return call(kernel, [(rows.shape, BF16)], rows, flops=2**20)[0]


def add_piece(own, theirs, piece):
    block = own.shape[0] // (2 * PIECES)
    shape = (block, own.shape[1])

    def kernel(own_ref, theirs_ref, kept_ref, given_ref):
        for i, out_ref in enumerate((kept_ref, given_ref)):
            rows = pl.ds((2 * piece + i) * block, block)
            total = own_ref[rows] + theirs_ref[rows].astype(F32)
            out_ref[...] = total.astype(out_ref.dtype)

    return call(kernel, [(shape, F32), (shape, BF16)], own, theirs, flops=2**20)


def add(kept, got, kinds):
    def kernel(kept_ref, got_ref, *out_refs):
        total = kept_ref[...] + got_ref[...].astype(F32)
        for out_ref in out_refs:
            out_ref[...] = total.astype(out_ref.dtype)

    return call(kernel, [(kept.shape, kind) for kind in kinds], kept, got, flops=2**20)


def sum_scores(theirs, own):
    theirs = swap(theirs, "c", 1)
    mine, other = [], []
    for piece in range(PIECES):
        kept, given = add_piece(own, theirs, piece)
        kept, given = add(kept, swap(given, "z", 1), (F32, BF16))
        (whole,) = add(kept, swap(given, "z", 2), (BF16,))
        arrived = swap(whole, "z", 1)
        mine += [whole, swap(whole, "c", 1)]
        other += [arrived, swap(arrived, "c", 1)]
    return mine, other


def product_term(x_refs, s_refs, share, cols):
    total = None
    for i, s_ref in enumerate(s_refs):
        x_ref = x_refs[i % 2]
        rows = token_rows(x_ref)[i // 2 * 2 + share]
        term = dot(s_ref[...], x_ref[rows, cols], 0, 0)
        total = term if total is None else total + term
    return total


def product_mine(x_own, x_theirs, scores):
    features = x_own.shape[1]
    tokens, probes = scores[0].shape

    def kernel(xo_ref, xt_ref, *refs):
        *s_refs, y_ref = refs
        for i in range(0, features, TILE):
            cols = pl.ds(i, TILE)
            y_ref[:, cols] = product_term((xo_ref, xt_ref), s_refs, 0, cols)

    return call(
        kernel,
        [((probes, features), F32)],
        x_own,
        x_theirs,
        *scores,
        flops=2 * len(scores) * tokens * features * probes,
    )[0]


def product_all(y_mine, x_own, x_theirs, scores):
    features = x_own.shape[1]
    tokens, probes = scores[0].shape

    def kernel(y_ref, xo_ref, xt_ref, *refs):
        *s_refs, kept_ref, given_ref, sum_ref, order_ref = refs
        for i in range(0, features, TILE):
            cols = pl.ds(i, TILE)
            term = product_term((xo_ref, xt_ref), s_refs, 1, cols)
            sum_ref[:, cols] = y_ref[:, cols] + term
        reorder(sum_ref, order_ref)
        kept_ref[...] = order_ref[pl.ds(0, probes // 4)]
        for i in range(3):
            rows = pl.ds((i + 1) * (probes // 4), probes // 4)
            given_ref[i] = order_ref[rows].astype(BF16)

    return call(
        kernel,
        [((probes // 4, features), F32), ((3, probes // 4, features), BF16)],
        y_mine,
        x_own,
        x_theirs,
        *scores,
        scratch=[pltpu.VMEM((probes, features), F32)] * 2,
        flops=2 * len(scores) * tokens * features * probes,
    )


def product(x_theirs, x_own, scores):
    mine, other = scores
    y = product_mine(x_own, x_theirs, mine)
    kept, given = product_all(y, x_own, x_theirs, other)
    total = reduce_four(kept, given, 0).reshape(4, ROWS, -1)
    return reduce_four(total[0], total[1:].astype(BF16), 1)


def spread(rounded):
    part = gather_four(rounded, 1).reshape(4 * ROWS, -1)
    full = gather_four(part, 0).reshape(16 * ROWS, -1)
    return in_order_a(full)


def shards(activations, probes):
    h = lax.axis_index("h")
    total_tokens = activations.shape[0] * 32

    x_theirs, x_own, mine, theirs = load(activations, probes)
    scores = sum_scores(theirs, score(x_own, mine, F32))
    rows = product(x_theirs, x_own, scores)
    rows = (rows + swap(rows.astype(BF16), "h", 1).astype(F32)) / total_tokens
    first = lax.dynamic_slice_in_dim(rows, h * 8, 8, 0)

    full = spread(rows.astype(BF16))
    theirs = score(x_theirs, full, BF16)
    own = score(x_own, full, F32)
    rows = product(x_theirs, x_own, sum_scores(theirs, own))
    mine = lax.dynamic_slice_in_dim(rows, h * 8, 8, 0)
    other = lax.dynamic_slice_in_dim(rows, (1 - h) * 8, 8, 0)
    return first, (mine + swap(other, "h", 1)) / total_tokens


def solution(mesh):
    split = Mesh(mesh.devices.reshape(tuple(SIZES.values())), tuple(SIZES))
    tok, feat = ("x", "h", "y"), ("z", "c")
    return jax.shard_map(
        shards,
        mesh=split,
        in_specs=(P(tok, feat), P(None, feat)),
        out_specs=(P(tok, feat), P(tok, feat)),
        check_vma=False,
    )
```

```python
import jax
import jax.numpy as jnp
from jax import lax
from jax.experimental import pallas as pl
from jax.experimental.pallas import tpu as pltpu
from jax.sharding import Mesh, PartitionSpec as P

SIZES = {"x": 4, "h": 2, "y": 4, "z": 4, "c": 2}
F32, BF16 = jnp.float32, jnp.bfloat16
VMEM = pl.BlockSpec(memory_space=pltpu.VMEM)
TILE = 512

ROWS = 16
PIECES = 2


def dot(a, b, dim_a, dim_b):
    return lax.dot_general(
        a, b, (((dim_a,), (dim_b,)), ((), ())), preferred_element_type=F32
    )


def swap(value, axis, mask):
    return lax.ppermute(value, axis, [(i, i ^ mask) for i in range(SIZES[axis])])


def swap_xy(value, stage, bits):
    pairs = []
    for x in range(4):
        for y in range(4):
            for c in range(2):
                to = (x ^ bits) * 4 + y if c == stage else x * 4 + (y ^ bits)
                pairs.append(((x * 4 + y) * 2 + c, to * 2 + c))
    return lax.ppermute(value, ("x", "y", "c"), pairs)


def reduce_four(kept, given, stage):
    total = kept
    for got in [swap_xy(given[i - 1], stage, i) for i in (2, 1, 3)]:
        total = total + got.astype(F32)
    return total


def gather_four(part, stage):
    got = {i: swap_xy(part, stage, i) for i in (2, 1, 3)}
    return [part, got[1], got[2], got[3]]


def call(kernel, outs, *args, specs=None, scratch=(), flops=0, limit=16):
    return pl.pallas_call(
        kernel,
        in_specs=specs or [VMEM] * len(args),
        out_specs=[VMEM] * len(outs),
        out_shape=[pltpu.VMEM(shape, kind) for shape, kind in outs],
        scratch_shapes=list(scratch),
        compiler_params=pltpu.CompilerParams(vmem_limit_bytes=limit * 2**20),
        cost_estimate=pl.CostEstimate(
            flops=flops, bytes_accessed=2**20, transcendentals=0
        ),
    )(*args)


def token_rows(x_ref):
    parity = lax.rem(lax.axis_index("z"), 2)
    block = x_ref.shape[0] // (2 * PIECES)
    starts = []
    for piece in range(PIECES):
        for chip in (parity, 1 - parity):
            starts.append((chip * PIECES + piece) * block)
    return [pl.ds(pl.multiple_of(start, block), block) for start in starts]


def write_scores(x_ref, probes, s_ref):
    block = x_ref.shape[0] // (2 * PIECES)
    for i, rows in enumerate(token_rows(x_ref)):
        value = dot(x_ref[rows], probes, 1, 1)
        s_ref[pl.ds(i * block, block)] = value.astype(s_ref.dtype)


def load(activations, probes):
    tokens, features = activations.shape
    half, count = tokens // 2, probes.shape[0]

    def kernel(x_hbm, p_hbm, theirs_ref, own_ref, p_ref, s_ref, raw_ref, row_ref, sems):
        core, x, y = (lax.axis_index(name) for name in ("c", "x", "y"))

        def rows_of(c):
            return x_hbm.at[pl.ds(pl.multiple_of(c * half, half), half)]

        copies = [
            pltpu.make_async_copy(p_hbm, raw_ref, sems.at[0]),
            pltpu.make_async_copy(rows_of(1 - core), theirs_ref, sems.at[1]),
            pltpu.make_async_copy(rows_of(core), own_ref, sems.at[2]),
        ]
        for copy in copies:
            copy.start()
        copies[0].wait()
        row_ref[...] = raw_ref[...].astype(F32)
        for i in range(16):
            at_x = lax.bitwise_xor(x, i // 4)
            at_y = lax.bitwise_xor(y, i % 4)
            pair = [
                row_ref[pl.ds(pl.multiple_of(at_x * 64 + h * 32 + at_y * 8, 8), 8)]
                for h in range(2)
            ]
            p_ref[pl.ds(i * ROWS, ROWS)] = jnp.concatenate(pair, 0).astype(BF16)
        copies[1].wait()
        write_scores(theirs_ref, p_ref[...], s_ref)
        copies[2].wait()

    hbm = pl.BlockSpec(memory_space=pltpu.HBM)
    return call(
        kernel,
        [((half, features), BF16)] * 2 + [(probes.shape, BF16), ((half, count), BF16)],
        activations,
        probes,
        specs=[hbm, hbm],
        scratch=[
            pltpu.VMEM(probes.shape, BF16),
            pltpu.VMEM(probes.shape, F32),
            pltpu.SemaphoreType.DMA((3,)),
        ],
        flops=tokens * features * count,
        limit=48,
    )


def score(x_half, probes, out_type):
    tokens, features = x_half.shape

    def kernel(x_ref, p_ref, s_ref):
        write_scores(x_ref, p_ref[...], s_ref)

    return call(
        kernel,
        [((tokens, probes.shape[0]), out_type)],
        x_half,
        probes,
        flops=2 * tokens * features * probes.shape[0],
    )[0]


def reorder(ref, out_ref):
    core = lax.axis_index("c")

    @pl.when(core == 0)
    def _():
        out_ref[...] = ref[...]

    @pl.when(core == 1)
    def _():
        blocks = [
            ref[pl.ds((inner * 4 + outer) * ROWS, ROWS)]
            for outer in range(4)
            for inner in range(4)
        ]
        out_ref[...] = jnp.concatenate(blocks, 0)


def in_order_a(parts):
    rows, features = parts[0].shape

    def kernel(*refs):
        *part_refs, out_ref = refs
        core = lax.axis_index("c")

        @pl.when(core == 0)
        def _():
            for outer, ref in enumerate(part_refs):
                out_ref[pl.ds(outer * rows, rows)] = ref[...]

        @pl.when(core == 1)
        def _():
            for outer, ref in enumerate(part_refs):
                for inner in range(4):
                    at = pl.ds((inner * 4 + outer) * ROWS, ROWS)
                    out_ref[at] = ref[pl.ds(inner * ROWS, ROWS)]

    return call(kernel, [((4 * rows, features), BF16)], *parts, flops=2**20)[0]


def add_piece(own, theirs, piece):
    block = own.shape[0] // (2 * PIECES)
    shape = (block, own.shape[1])

    def kernel(own_ref, theirs_ref, kept_ref, given_ref):
        for i, out_ref in enumerate((kept_ref, given_ref)):
            rows = pl.ds((2 * piece + i) * block, block)
            total = own_ref[rows] + theirs_ref[rows].astype(F32)
            out_ref[...] = total.astype(out_ref.dtype)

    return call(kernel, [(shape, F32), (shape, BF16)], own, theirs, flops=2**20)


def add(kept, got, kinds):
    def kernel(kept_ref, got_ref, *out_refs):
        total = kept_ref[...] + got_ref[...].astype(F32)
        for out_ref in out_refs:
            out_ref[...] = total.astype(out_ref.dtype)

    return call(kernel, [(kept.shape, kind) for kind in kinds], kept, got, flops=2**20)


def sum_scores(theirs, own):
    theirs = swap(theirs, "c", 1)
    mine, other = [], []
    for piece in range(PIECES):
        kept, given = add_piece(own, theirs, piece)
        kept, given = add(kept, swap(given, "z", 1), (F32, BF16))
        (whole,) = add(kept, swap(given, "z", 2), (BF16,))
        arrived = swap(whole, "z", 1)
        mine += [whole, swap(whole, "c", 1)]
        other += [arrived, swap(arrived, "c", 1)]
    return mine, other


def product_term(x_refs, s_refs, share, cols):
    total = None
    for i, s_ref in enumerate(s_refs):
        x_ref = x_refs[i % 2]
        rows = token_rows(x_ref)[i // 2 * 2 + share]
        term = dot(s_ref[...], x_ref[rows, cols], 0, 0)
        total = term if total is None else total + term
    return total


def product_mine(x_own, x_theirs, scores):
    features = x_own.shape[1]
    tokens, probes = scores[0].shape

    def kernel(xo_ref, xt_ref, *refs):
        *s_refs, y_ref = refs
        for i in range(0, features, TILE):
            cols = pl.ds(i, TILE)
            y_ref[:, cols] = product_term((xo_ref, xt_ref), s_refs, 0, cols)

    return call(
        kernel,
        [((probes, features), F32)],
        x_own,
        x_theirs,
        *scores,
        flops=2 * len(scores) * tokens * features * probes,
    )[0]


def product_all(y_mine, x_own, x_theirs, scores):
    features = x_own.shape[1]
    tokens, probes = scores[0].shape

    def kernel(y_ref, xo_ref, xt_ref, *refs):
        *s_refs, kept_ref, given_ref, sum_ref, order_ref = refs
        for i in range(0, features, TILE):
            cols = pl.ds(i, TILE)
            term = product_term((xo_ref, xt_ref), s_refs, 1, cols)
            sum_ref[:, cols] = y_ref[:, cols] + term
        reorder(sum_ref, order_ref)
        kept_ref[...] = order_ref[pl.ds(0, probes // 4)]
        for i in range(3):
            rows = pl.ds((i + 1) * (probes // 4), probes // 4)
            given_ref[i] = order_ref[rows].astype(BF16)

    return call(
        kernel,
        [((probes // 4, features), F32), ((3, probes // 4, features), BF16)],
        y_mine,
        x_own,
        x_theirs,
        *scores,
        scratch=[pltpu.VMEM((probes, features), F32)] * 2,
        flops=2 * len(scores) * tokens * features * probes,
    )


def product(x_theirs, x_own, scores):
    mine, other = scores
    y = product_mine(x_own, x_theirs, mine)
    kept, given = product_all(y, x_own, x_theirs, other)
    total = reduce_four(kept, given, 0).reshape(4, ROWS, -1)
    return reduce_four(total[0], total[1:].astype(BF16), 1)


def spread(rounded):
    part = jnp.concatenate(gather_four(rounded, 1), 0)
    return in_order_a(gather_four(part, 0))


def shards(activations, probes):
    h = lax.axis_index("h")
    total_tokens = activations.shape[0] * 32

    x_theirs, x_own, mine, theirs = load(activations, probes)
    scores = sum_scores(theirs, score(x_own, mine, F32))
    rows = product(x_theirs, x_own, scores)
    rows = (rows + swap(rows.astype(BF16), "h", 1).astype(F32)) / total_tokens
    first = lax.dynamic_slice_in_dim(rows, h * 8, 8, 0)

    full = spread(rows.astype(BF16))
    theirs = score(x_theirs, full, BF16)
    own = score(x_own, full, F32)
    rows = product(x_theirs, x_own, sum_scores(theirs, own))
    mine = lax.dynamic_slice_in_dim(rows, h * 8, 8, 0)
    other = lax.dynamic_slice_in_dim(rows, (1 - h) * 8, 8, 0)
    return first, (mine + swap(other, "h", 1)) / total_tokens


def solution(mesh):
    split = Mesh(mesh.devices.reshape(tuple(SIZES.values())), tuple(SIZES))
    tok, feat = ("x", "h", "y"), ("z", "c")
    return jax.shard_map(
        shards,
        mesh=split,
        in_specs=(P(tok, feat), P(None, feat)),
        out_specs=(P(tok, feat), P(tok, feat)),
        check_vma=False,
    )
```
